32 devices in a mesh: dp: 8 (over y, x, core), mp: 4 (over z).
Axes of the slice: x: 2, y: 2, z: 4, core: 2. Of those that a mesh axis runs over, the one named last changes fastest.
Arguments:
- hidden: bfloat16 [128, 1024], P('dp'), may hold values from -6 to 6
- attn_gain: float32 [1024], replicated, may hold values from 0.25 to 1.75
- w_qkv: bfloat16 [1024, 3, 1024], P(None, None, 'mp'), may hold values from -2 to 2
- w_out: bfloat16 [1024, 1024], P('mp'), may hold values from -0.1875 to 0.1875
- mlp_gain: float32 [1024], replicated, may hold values from 0.25 to 1.75
- w_gate_up: bfloat16 [1024, 2, 4096], P(None, None, 'mp'), may hold values from -0.1875 to 0.1875
- w_down: bfloat16 [4096, 1024], P('mp'), may hold values from -0.09375 to 0.09375
- kv_cache: bfloat16 [2, 1024, 128, 1024], P(None, 'dp', None, 'mp'), may hold values from -9 to 9
- lengths: int32 [128], replicated, may hold values from 1 to 16384, as said below
- page_request: int32 [1024], P('dp'), may hold values from -1 to 127, as said below
- page_index: int32 [1024], P('dp'), may hold values from 0 to 127, as said below
Outputs:
- appended: bfloat16 [2, 128, 1024], P(None, 'dp', 'mp')
- hidden_out: bfloat16 [128, 1024], P('dp')
The draws below stay inside these ranges and needn't reach their ends.
Inputs may be any that keep to these rules, and one draw needn't show every extreme that they name: `lengths`: 1 request hold exactly 16384 tokens, the others fewer than 512. `page_request`: each request owns exactly ceil(lengths / 128) pool pages, which may lie on any data devices; -1 marks an empty page. `page_index`: the pages of a request carry the places 0 to ceil(lengths / 128) - 1, each once; empty pages carry 0.
All inputs are finite; a program needn't handle non-finite values.
Results may differ from the reference program's by a relative error of at most 0.0085.
Values may be sent and summed in bfloat16 or wider, within the bound.
A program may use at most 128 MiB of HBM per device.

```python
import math
import jax
import jax.numpy as jnp
from jax import lax

D = 1024
FF = 4096
HEADS = 16
HEAD_DIM = 64
PAGE = 128
MAX_PAGES = 128
POOL = 128
REQS = 128
TOTAL_PAGES = 1024
LONG = 1


def paged_plan(key):
    base_key = jax.random.fold_in(key, 7103)
    k_level, k_offset, k_long, k_bias, k_jitter = jax.random.split(base_key, 5)
    top_level = (4 * PAGE).bit_length() - 1
    levels = jax.random.randint(k_level, (REQS,), 0, top_level)
    level_base = jnp.left_shift(jnp.int32(1), levels)
    short_len = level_base + jax.random.randint(k_offset, (REQS,), 0, 1 << 20) % level_base
    chosen = jax.random.permutation(k_long, REQS)[:LONG]
    is_long = jnp.zeros((REQS,), jnp.int32).at[chosen].set(1)
    lengths = jnp.where(is_long > 0, MAX_PAGES * PAGE, short_len).astype(jnp.int32)
    page_counts = (lengths + PAGE - 1) // PAGE
    page_ends = jnp.cumsum(page_counts)
    page_starts = page_ends - page_counts
    used_pages = page_ends[-1]
    devices = TOTAL_PAGES // POOL
    device_bias = jax.random.randint(k_bias, (devices,), 0, 4)
    jitters = jax.random.randint(k_jitter, (TOTAL_PAGES,), 0, 1024)
    slot_ids = jnp.arange(TOTAL_PAGES, dtype=jnp.int32)
    priority = (device_bias[slot_ids // POOL] * 1024 + jitters) * 16384 + slot_ids
    visit = jnp.argsort(priority)
    slot_rank = jnp.argsort(visit).astype(jnp.int32)
    owner_ids = jnp.searchsorted(page_ends, slot_rank, side='right').astype(jnp.int32)
    clamped = jnp.minimum(owner_ids, REQS - 1)
    filled = slot_rank < used_pages
    request_ids = jnp.where(filled, clamped, -1).astype(jnp.int32)
    page_places = jnp.where(filled, slot_rank - page_starts[clamped], 0).astype(jnp.int32)
    return (lengths, request_ids, page_places)


def draw_lengths(key, part):
    return paged_plan(key)[0]


def draw_page_request(key, part):
    return paged_plan(key)[1]


def draw_page_index(key, part):
    return paged_plan(key)[2]


def special_heads(key):
    head_order = jax.random.permutation(jax.random.fold_in(key, 5309), HEADS)
    chosen_count = max(1, HEADS // 4)
    head_flags = jnp.zeros((HEADS,), jnp.float32).at[head_order[:chosen_count]].set(1.0)
    return head_flags


def draw_w_qkv(key, part):
    head_flags = special_heads(key)
    column_flags = jnp.repeat(head_flags, HEAD_DIM)
    query_flags = (jnp.arange(3) == 0).astype(jnp.float32)
    random_key = jax.random.fold_in(key, 811)
    full_shape = (D, 3, HEADS * HEAD_DIM)
    random_part = jnp.clip(jax.random.normal(random_key, full_shape, jnp.float32), -4.0, 4.0)
    strength = 25.0
    offset = strength / math.sqrt(D * HEAD_DIM)
    return (random_part / math.sqrt(D) + offset * query_flags[None, :, None] * column_flags[None, None, :]).astype(jnp.bfloat16)


def draw_kv_cache(key, part):
    head_flags = special_heads(key)
    base_key = jax.random.fold_in(key, 2203)
    pick_key, random_key = jax.random.split(base_key)
    aligned = (jax.random.randint(pick_key, (TOTAL_PAGES, PAGE, HEADS), 0, 16) == 0).astype(jnp.float32) * head_flags
    full_shape = (2, TOTAL_PAGES, PAGE, HEADS, HEAD_DIM)
    random_part = jnp.clip(jax.random.normal(random_key, full_shape, jnp.float32), -4.5, 4.5)
    raised = 4.0
    slot_flags = (jnp.arange(2) == 0).astype(jnp.float32)
    lifted = random_part + raised * slot_flags[:, None, None, None, None] * aligned[None, :, :, :, None]
    return lifted.reshape(2, TOTAL_PAGES, PAGE, HEADS * HEAD_DIM).astype(jnp.bfloat16)


def block_levels(stream_key, dims, cuts, smallest, top_value):
    def one(axis_at, shards_of):
        draws = jax.random.uniform(jax.random.fold_in(jax.random.fold_in(stream_key, 6), axis_at), (shards_of,), jnp.float32, smallest / len(cuts), top_value / len(cuts))
        return jnp.repeat(jnp.exp(draws), dims[axis_at] // shards_of).reshape((-1,) + (1,) * (len(dims) - axis_at - 1))

    factor_of = one(*cuts[0])
    for cut in cuts[1:]:
        factor_of = factor_of * one(*cut)
    return factor_of


def normal_values(rng, dims, deviation, reach, cuts=(), held_as=jnp.bfloat16):
    array = deviation * jax.random.normal(rng, dims, jnp.float32)
    if cuts:
        array = array * block_levels(rng, dims, cuts, -0.22, 0.18)
    return jnp.clip(array, -reach, reach).astype(held_as)


def setup_inputs(seed: int = 0) -> dict:
    key_list = jax.random.split(jax.random.key(seed), 12)
    hidden = normal_values(key_list[0], (REQS, D), 1.0, 6.0, ((0, 8),))
    attn_gain = jnp.clip(1.0 + 0.15 * jax.random.normal(key_list[1], (D,), jnp.float32), 0.25, 1.75)
    w_qkv = draw_w_qkv(jax.random.fold_in(key_list[11], 71), 0)
    w_out = normal_values(key_list[3], (HEADS * HEAD_DIM, D), (HEADS * HEAD_DIM) ** -0.5, 0.1875, ((0, 4),))
    mlp_gain = jnp.clip(1.0 + 0.15 * jax.random.normal(key_list[4], (D,), jnp.float32), 0.25, 1.75)
    w_gate_up = normal_values(key_list[5], (D, 2, FF), D ** -0.5, 0.1875, ((2, 4),))
    w_down = normal_values(key_list[6], (FF, D), FF ** -0.5, 0.09375, ((0, 4),))
    kv_cache = draw_kv_cache(jax.random.fold_in(key_list[11], 71), 0)
    lengths = draw_lengths(jax.random.fold_in(key_list[11], 71), 0)
    page_request = draw_page_request(jax.random.fold_in(key_list[11], 71), 0)
    page_index = draw_page_index(jax.random.fold_in(key_list[11], 71), 0)
    return {"hidden": hidden, "attn_gain": attn_gain, "w_qkv": w_qkv, "w_out": w_out, "mlp_gain": mlp_gain, "w_gate_up": w_gate_up, "w_down": w_down, "kv_cache": kv_cache, "lengths": lengths, "page_request": page_request, "page_index": page_index}


EPSILON = 1e-05
NEGATIVE = -1e+30

def rms_norm(values, gain):
    widened = values.astype(jnp.float32)
    mean_square = lax.optimization_barrier(jnp.mean(widened * widened, axis=-1, keepdims=True))
    return (widened * lax.rsqrt(mean_square + EPSILON) * gain).astype(jnp.bfloat16)

def reference(hidden, attn_gain, w_qkv, w_out, mlp_gain, w_gate_up, w_down, kv_cache, lengths, page_request, page_index):
    head_cols = HEADS * HEAD_DIM
    score_scale = HEAD_DIM ** (-0.5)
    normed = rms_norm(hidden, attn_gain)
    projected = jnp.dot(normed, w_qkv.reshape(D, 3 * head_cols), preferred_element_type=jnp.float32)
    projected = lax.optimization_barrier(projected.astype(jnp.bfloat16)).reshape(REQS, 3, head_cols)
    appended = jnp.stack([projected[:, 1], projected[:, 2]])
    queries = projected[:, 0].reshape(REQS, HEADS, HEAD_DIM).astype(jnp.float32)
    new_keys = projected[:, 1].reshape(REQS, HEADS, HEAD_DIM).astype(jnp.float32)
    new_values = projected[:, 2].reshape(REQS, HEADS, HEAD_DIM).astype(jnp.float32)
    self_scores = lax.optimization_barrier(jnp.sum(queries * new_keys, axis=-1)) * score_scale
    request_ids = jnp.arange(REQS, dtype=jnp.int32)
    offsets = jnp.arange(PAGE, dtype=jnp.int32)

    def block_pages(block_index):
        start = block_index * POOL
        fetched = lax.dynamic_slice_in_dim(kv_cache, start, POOL, 1)
        key_rows = fetched[0].reshape(POOL, PAGE, HEADS, HEAD_DIM).astype(jnp.float32)
        value_rows = fetched[1].reshape(POOL, PAGE, HEADS, HEAD_DIM).astype(jnp.float32)
        owners = lax.dynamic_slice_in_dim(page_request, start, POOL, 0)
        page_pos = lax.dynamic_slice_in_dim(page_index, start, POOL, 0)
        clamped = jnp.maximum(owners, 0)
        scores = jnp.einsum('phd,pthd->pht', queries[clamped], key_rows) * score_scale
        position = page_pos[:, None] * PAGE + offsets[None, :]
        usable = (owners[:, None] >= 0) & (position < lengths[clamped][:, None])
        page_max = lax.optimization_barrier(jnp.max(jnp.where(usable[:, None, :], scores, NEGATIVE), axis=2))
        member = owners[:, None] == request_ids[None, :]
        return (scores, usable, page_max, value_rows, member, clamped, owners)

    def max_step(running_max, block_index):
        scores, usable, page_max, value_rows, member, clamped, owners = block_pages(block_index)
        candidate = lax.optimization_barrier(jnp.max(jnp.where(member[:, :, None], page_max[:, None, :], NEGATIVE), axis=0))
        return (jnp.maximum(running_max, candidate), None)
    blocks = jnp.arange(TOTAL_PAGES // POOL, dtype=jnp.int32)
    running_max, _ = lax.scan(max_step, self_scores, blocks)

    def sum_step(carry, block_index):
        totals, weighted = carry
        scores, usable, page_max, value_rows, member, clamped, owners = block_pages(block_index)
        raw = jnp.where(usable[:, None, :], jnp.exp(scores - page_max[:, :, None]), 0.0)
        page_total = lax.optimization_barrier(jnp.sum(raw, axis=2))
        rounded = lax.optimization_barrier(raw.astype(jnp.bfloat16)).astype(jnp.float32)
        page_sum = jnp.einsum('pht,pthd->phd', rounded, value_rows)
        factors = jnp.where(owners[:, None] >= 0, jnp.exp(page_max - running_max[clamped]), 0.0)
        onehot = member.astype(jnp.float32)
        totals = totals + jnp.einsum('pr,ph->rh', onehot, page_total * factors, precision=lax.Precision.HIGHEST)
        weighted = weighted + jnp.einsum('pr,phd->rhd', onehot, page_sum * factors[:, :, None], precision=lax.Precision.HIGHEST)
        return ((totals, weighted), None)
    self_weight = jnp.exp(self_scores - running_max)
    (totals, weighted), _ = lax.scan(sum_step, (self_weight, self_weight[:, :, None] * new_values), blocks)
    context = (weighted / totals[:, :, None]).reshape(REQS, head_cols).astype(jnp.bfloat16)
    attended = jnp.dot(context, w_out, preferred_element_type=jnp.float32)
    residual = lax.optimization_barrier((hidden.astype(jnp.float32) + attended).astype(jnp.bfloat16))
    normed_mlp = rms_norm(residual, mlp_gain)
    gate_up = jnp.dot(normed_mlp, w_gate_up.reshape(D, 2 * FF), preferred_element_type=jnp.float32).reshape(REQS, 2, FF)
    activated = (jax.nn.silu(gate_up[:, 0]) * gate_up[:, 1]).astype(jnp.bfloat16)
    lowered = jnp.dot(activated, w_down, preferred_element_type=jnp.float32)
    hidden_out = (residual.astype(jnp.float32) + lowered).astype(jnp.bfloat16)
    return (appended, hidden_out)
```

```python
import functools

import jax
import jax.numpy as jnp
from jax import lax
from jax.experimental import pallas as pl
from jax.experimental.pallas import tpu as pltpu
from jax.sharding import PartitionSpec as P

HEAD_DIM = 64
CHUNK = 8
LANES = 128
EPSILON = 1e-05
NEGATIVE = -1e30
F32 = jnp.float32
BF16 = jnp.bfloat16


def rms_norm(values, gain):
    widened = values.astype(F32)
    mean_square = jnp.mean(widened * widened, axis=-1, keepdims=True)
    return (widened * lax.rsqrt(mean_square + EPSILON) * gain).astype(BF16)


def dot(a, b):
    return jnp.dot(a, b, preferred_element_type=F32)


def kernel(
    n_dp,
    n_mp,
    hidden,
    attn_gain,
    w_qkv_hbm,
    w_out_hbm,
    mlp_gain,
    w_gu_hbm,
    w_down_hbm,
    kv_hbm,
    lengths,
    owners,
    places,
    appended,
    hidden_out,
    w_qkv,
    w_out,
    w_gu,
    w_down,
    kv,
    queries,
    partial_out,
    partial_in,
    sums_one,
    sums_two,
    page_query,
    bias,
    page_stats,
    page_sum,
    w_sem,
    kv_sem,
    q_send,
    q_recv,
    p_send,
    p_recv,
    s_send,
    s_recv,
):
    rows, width = hidden.shape
    cols = w_qkv.shape[2]
    heads = cols // HEAD_DIM
    pages, page_len = kv.shape[1], kv.shape[2]
    requests = rows * n_dp
    chunks = pages // CHUNK
    me_dp = lax.axis_index("dp")
    me_mp = lax.axis_index("mp")

    w_copies = [
        pltpu.make_async_copy(src, dst, w_sem.at[i])
        for i, (src, dst) in enumerate(
            ((w_qkv_hbm, w_qkv), (w_out_hbm, w_out), (w_gu_hbm, w_gu), (w_down_hbm, w_down))
        )
    ]
    w_copies[0].start()

    def kv_copy(c):
        at = pl.ds(c * CHUNK, CHUNK)
        return pltpu.make_async_copy(kv_hbm.at[:, at], kv.at[:, at], kv_sem.at[c])

    barrier = pltpu.get_barrier_semaphore()
    for k in range(1, n_dp):
        pl.semaphore_signal(
            barrier,
            inc=1,
            device_id=(lax.rem(me_dp + k, n_dp), me_mp),
            device_id_type=pl.DeviceIdType.MESH,
        )
    for k in range(1, n_mp):
        pl.semaphore_signal(
            barrier,
            inc=1,
            device_id=(me_dp, lax.rem(me_mp + k, n_mp)),
            device_id_type=pl.DeviceIdType.MESH,
        )
    lax.fori_loop(0, chunks, lambda c, _: kv_copy(c).start(), None)
    for copy in w_copies[1:]:
        copy.start()

    normed = rms_norm(hidden[...], attn_gain[...])
    w_copies[0].wait()
    own_query, own_key, own_value = (dot(normed, w_qkv[i]).astype(BF16) for i in range(3))
    appended[0] = own_key
    appended[1] = own_value
    queries[me_dp] = own_query
    pl.semaphore_wait(barrier, n_dp + n_mp - 2)

    def query_copy(k, slot):
        return pltpu.make_async_remote_copy(
            src_ref=queries.at[slot],
            dst_ref=queries.at[slot],
            send_sem=q_send.at[k],
            recv_sem=q_recv.at[k],
            device_id=(lax.rem(me_dp + k, n_dp), me_mp),
            device_id_type=pl.DeviceIdType.MESH,
        )

    for k in range(1, n_dp):
        query_copy(k, me_dp).start()

    owner_row = owners[...]
    owner_by_request = jnp.broadcast_to(owner_row, (requests, pages))
    member_rp = owner_by_request == lax.broadcasted_iota(jnp.int32, (requests, pages), 0)
    owner_by_page = jnp.transpose(owner_by_request.astype(F32))
    member_pr = owner_by_page == lax.broadcasted_iota(jnp.int32, (pages, requests), 1).astype(F32)
    page_length = jnp.sum(jnp.where(member_pr, lengths[...].astype(F32), 0.0), axis=1, keepdims=True)
    place = jnp.transpose(jnp.broadcast_to(places[...], (page_len, pages)).astype(F32))
    token = lax.broadcasted_iota(jnp.int32, (pages, page_len), 1).astype(F32)
    bias[...] = jnp.where(place * page_len + token < page_length, 0.0, NEGATIVE)

    lane = lax.broadcasted_iota(jnp.int32, (rows, LANES), 1)
    product = own_query.astype(F32) * own_key.astype(F32)
    self_lse = jnp.full((rows, LANES), NEGATIVE, F32)
    for h in range(heads):
        score = jnp.sum(product[:, h * HEAD_DIM : (h + 1) * HEAD_DIM], axis=1, keepdims=True)
        self_lse = jnp.where(lane == h, score * HEAD_DIM**-0.5, self_lse)

    for k in range(1, n_dp):
        query_copy(k, lax.rem(me_dp + n_dp - k, n_dp)).wait_recv()
    every_query = queries[...].reshape(requests, cols)
    page_query[...] = dot(member_pr.astype(F32).astype(BF16), every_query) * HEAD_DIM**-0.5

    head_mask = (
        lax.broadcasted_iota(jnp.int32, (8, cols), 1) // HEAD_DIM
        == lax.broadcasted_iota(jnp.int32, (8, cols), 0)
    ).astype(F32)
    half = lax.broadcasted_iota(jnp.int32, (8, LANES), 1) < LANES // 2

    def visit(c, _):
        kv_copy(c).wait()
        for j in range(CHUNK):
            p = c * CHUNK + j
            query = (page_query[pl.ds(p, 1), :] * head_mask).astype(BF16)
            dead = bias[pl.ds(p, 1), :]
            scores = (
                lax.dot_general(
                    query, kv[0, p], (((1,), (1,)), ((), ())), preferred_element_type=F32
                )
                + dead
            )
            largest = jnp.max(scores, axis=1, keepdims=True)
            raw = jnp.where(dead < 0.0, 0.0, jnp.exp(scores - largest))
            total = jnp.sum(raw, axis=1, keepdims=True)
            page_stats[p] = jnp.where(half, largest, total)
            values = dot(raw.astype(BF16), kv[1, p]) * head_mask
            page_sum[pl.ds(p, 1), :] = jnp.sum(values, axis=0, keepdims=True)
        return None

    lax.fori_loop(0, chunks, visit, None)

    part = lax.broadcasted_iota(jnp.int32, (requests, cols), 1) // HEAD_DIM
    stat_lane = lax.broadcasted_iota(jnp.int32, (requests, LANES), 1)
    factor_part = lax.broadcasted_iota(jnp.int32, (cols, pages), 0) // HEAD_DIM
    factors = jnp.zeros((cols, pages), F32)
    inverse = jnp.zeros((requests, cols), F32)
    lse = jnp.full((requests, LANES), NEGATIVE, F32)
    for h in range(heads):
        stats = jnp.transpose(page_stats[:, h, :])
        max_row = stats[0:1, :]
        total_row = stats[LANES // 2 : LANES // 2 + 1, :]
        top = jnp.max(jnp.where(member_rp, max_row, NEGATIVE), axis=1, keepdims=True)
        top_row = jnp.sum(jnp.where(member_rp, top, 0.0), axis=0, keepdims=True)
        factor = jnp.where(owner_row >= 0, jnp.exp(jnp.minimum(max_row - top_row, 0.0)), 0.0)
        total = jnp.sum(jnp.where(member_rp, factor * total_row, 0.0), axis=1, keepdims=True)
        filled = total > 0.0
        safe = jnp.where(filled, total, 1.0)
        factors = jnp.where(factor_part == h, factor, factors)
        inverse = jnp.where(part == h, 1.0 / safe, inverse)
        lse = jnp.where(
            stat_lane == h, jnp.where(filled, top + jnp.log(safe), NEGATIVE), lse
        )
    scaled = page_sum[...] * jnp.transpose(factors)
    high = scaled.astype(BF16)
    low = (scaled - high.astype(F32)).astype(BF16)
    member = member_rp.astype(F32).astype(BF16)
    local = (dot(member, high) + dot(member, low)) * inverse
    partial_out[:, :, 0:cols] = local.reshape(n_dp, rows, cols)
    partial_out[:, :, cols : cols + LANES] = lse.reshape(n_dp, rows, LANES)

    def partial_copy(k):
        to = lax.rem(me_dp + k, n_dp)
        return pltpu.make_async_remote_copy(
            src_ref=partial_out.at[to],
            dst_ref=partial_in.at[k],
            send_sem=p_send.at[k],
            recv_sem=p_recv.at[k],
            device_id=(to, me_mp),
            device_id_type=pl.DeviceIdType.MESH,
        )

    for k in range(1, n_dp):
        partial_copy(k).start()
    partial_in[0] = partial_out[me_dp]
    for k in range(1, n_dp):
        partial_copy(k).wait_recv()

    lses = partial_in[:, :, cols : cols + LANES]
    top = jnp.maximum(self_lse, jnp.max(lses, axis=0))
    self_share = jnp.exp(self_lse - top)
    shares = jnp.exp(lses - top[None])
    total = self_share + jnp.sum(shares, axis=0)
    column = lax.broadcasted_iota(jnp.int32, (rows, cols), 1) // HEAD_DIM

    def widen(share):
        wide = jnp.zeros((rows, cols), F32)
        for h in range(heads):
            wide = jnp.where(column == h, share[:, h : h + 1], wide)
        return wide

    weighted = widen(self_share) * own_value.astype(F32)
    for k in range(n_dp):
        weighted = weighted + widen(shares[k]) * partial_in[k, :, 0:cols]
    context = (weighted / widen(total)).astype(BF16)

    def sum_over_mp(term, slots, at):
        slots[me_mp] = term.astype(BF16)

        def copy(k, slot):
            return pltpu.make_async_remote_copy(
                src_ref=slots.at[slot],
                dst_ref=slots.at[slot],
                send_sem=s_send.at[at, k],
                recv_sem=s_recv.at[at, k],
                device_id=(me_dp, lax.rem(me_mp + k, n_mp)),
                device_id_type=pl.DeviceIdType.MESH,
            )

        for k in range(1, n_mp):
            copy(k, me_mp).start()
        for k in range(1, n_mp):
            copy(k, lax.rem(me_mp + n_mp - k, n_mp)).wait_recv()
        for k in range(1, n_mp):
            copy(k, me_mp).wait_send()
        return jnp.sum(slots[...].astype(F32), axis=0)

    w_copies[1].wait()
    attended = sum_over_mp(dot(context, w_out[...]), sums_one, 0)
    residual = (hidden[...].astype(F32) + attended).astype(BF16)
    normed_mlp = rms_norm(residual, mlp_gain[...])

    tiles = width // LANES
    spread_from = lax.broadcasted_iota(jnp.int32, (LANES, 4 * LANES), 0)
    spread_to = lax.broadcasted_iota(jnp.int32, (LANES, 4 * LANES), 1)
    even = spread_to == 2 * spread_from
    odd = spread_to == 2 * LANES + 2 * spread_from + 1
    spread = (even | odd).astype(F32).astype(BF16)
    stacked = jnp.concatenate(
        [normed_mlp[:, i * LANES : (i + 1) * LANES] for i in range(tiles)], axis=0
    )
    apart = dot(stacked, spread).astype(BF16)
    w_copies[2].wait()
    gate_up = None
    for i in range(tiles):
        rows_i = apart[i * rows : (i + 1) * rows]
        left = jnp.concatenate([rows_i[:, : 2 * LANES], rows_i[:, 2 * LANES :]], axis=0)
        right = w_gu[i * LANES : (i + 1) * LANES].reshape(2 * LANES, w_gu.shape[2])
        step = dot(left, right)
        gate_up = step if gate_up is None else gate_up + step
    gate, up = gate_up[:rows], gate_up[rows:]
    activated = (gate / (1.0 + jnp.exp(-gate)) * up).astype(BF16)
    w_copies[3].wait()
    lowered = sum_over_mp(dot(activated, w_down[...]), sums_two, 1)
    hidden_out[...] = (residual.astype(F32) + lowered).astype(BF16)

    for k in range(1, n_dp):
        query_copy(k, me_dp).wait_send()
        partial_copy(k).wait_send()


def body(n_dp, n_mp, hidden, attn_gain, w_qkv, w_out, mlp_gain, w_gate_up, w_down, kv_cache, lengths, page_request, page_index):
    rows, width = hidden.shape
    cols = w_qkv.shape[2]
    pages, page_len = kv_cache.shape[1:3]
    vmem = pl.BlockSpec(memory_space=pltpu.VMEM)
    hbm = pl.BlockSpec(memory_space=pl.ANY)
    dma = pltpu.SemaphoreType.DMA
    w_qkv = jnp.transpose(w_qkv, (1, 0, 2))
    return pl.pallas_call(
        functools.partial(kernel, n_dp, n_mp),
        out_shape=(
            jax.ShapeDtypeStruct((2, rows, cols), BF16),
            jax.ShapeDtypeStruct((rows, width), BF16),
        ),
        in_specs=[vmem, vmem, hbm, hbm, vmem, hbm, hbm, hbm, vmem, vmem, vmem],
        out_specs=(vmem, vmem),
        scratch_shapes=[
            pltpu.VMEM(w_qkv.shape, BF16),
            pltpu.VMEM(w_out.shape, BF16),
            pltpu.VMEM(w_gate_up.shape, BF16),
            pltpu.VMEM(w_down.shape, BF16),
            pltpu.VMEM(kv_cache.shape, BF16),
            pltpu.VMEM((n_dp, rows, cols), BF16),
            pltpu.VMEM((n_dp, rows, cols + LANES), F32),
            pltpu.VMEM((n_dp, rows, cols + LANES), F32),
            pltpu.VMEM((n_mp, rows, width), BF16),
            pltpu.VMEM((n_mp, rows, width), BF16),
            pltpu.VMEM((pages, cols), F32),
            pltpu.VMEM((pages, page_len), F32),
            pltpu.VMEM((pages, 8, LANES), F32),
            pltpu.VMEM((pages, cols), F32),
            dma((4,)),
            dma((pages // CHUNK,)),
            dma((n_dp,)),
            dma((n_dp,)),
            dma((n_dp,)),
            dma((n_dp,)),
            dma((2, n_mp)),
            dma((2, n_mp)),
        ],
        compiler_params=pltpu.CompilerParams(
            collective_id=0, has_side_effects=True, vmem_limit_bytes=56 * 1024 * 1024
        ),
    )(
        hidden,
        attn_gain.reshape(1, width),
        w_qkv,
        w_out,
        mlp_gain.reshape(1, width),
        w_gate_up,
        w_down,
        kv_cache,
        lengths.reshape(1, -1),
        page_request.reshape(1, -1),
        page_index.reshape(1, -1),
    )


def solution(mesh):
    return jax.shard_map(
        functools.partial(body, mesh.shape["dp"], mesh.shape["mp"]),
        mesh=mesh,
        in_specs=(
            P("dp", None),
            P(),
            P(None, None, "mp"),
            P("mp", None),
            P(),
            P(None, None, "mp"),
            P("mp", None),
            P(None, "dp", None, "mp"),
            P(),
            P("dp"),
            P("dp"),
        ),
        out_specs=(P(None, "dp", "mp"), P("dp", None)),
        check_vma=False,
    )
```

```python
import functools

import jax
import jax.numpy as jnp
from jax import lax
from jax.experimental import pallas as pl
from jax.experimental.pallas import tpu as pltpu
from jax.sharding import PartitionSpec as P

HEAD_DIM = 64
CHUNK = 8
LANES = 128
EPSILON = 1e-05
NEGATIVE = -1e30
F32 = jnp.float32
BF16 = jnp.bfloat16


def rms_norm(values, gain):
    widened = values.astype(F32)
    mean_square = jnp.mean(widened * widened, axis=-1, keepdims=True)
    return (widened * lax.rsqrt(mean_square + EPSILON) * gain).astype(BF16)


def dot(a, b):
    return jnp.dot(a, b, preferred_element_type=F32)


def kernel(
    n_dp,
    n_mp,
    hidden,
    attn_gain,
    w_qkv_hbm,
    w_out_hbm,
    mlp_gain,
    w_gu_hbm,
    w_down_hbm,
    kv_hbm,
    lengths,
    owners,
    places,
    appended,
    hidden_out,
    w_qkv,
    w_out,
    w_gu,
    w_down,
    kv,
    queries,
    partial_out,
    partial_in,
    sums_one,
    sums_two,
    page_query,
    bias,
    page_stats,
    page_sum,
    w_sem,
    kv_sem,
    q_send,
    q_recv,
    p_send,
    p_recv,
    s_send,
    s_recv,
):
    rows, width = hidden.shape
    cols = w_qkv.shape[2]
    heads = cols // HEAD_DIM
    pages, page_len = kv.shape[1], kv.shape[2]
    requests = rows * n_dp
    chunks = pages // CHUNK
    me_dp = lax.axis_index("dp")
    me_mp = lax.axis_index("mp")

    w_copies = [
        pltpu.make_async_copy(src, dst, w_sem.at[i])
        for i, (src, dst) in enumerate(
            ((w_qkv_hbm, w_qkv), (w_out_hbm, w_out), (w_gu_hbm, w_gu), (w_down_hbm, w_down))
        )
    ]
    w_copies[0].start()

    def kv_copy(c):
        at = pl.ds(c * CHUNK, CHUNK)
        return pltpu.make_async_copy(kv_hbm.at[:, at], kv.at[:, at], kv_sem.at[c])

    barrier = pltpu.get_barrier_semaphore()
    for k in range(1, n_dp):
        pl.semaphore_signal(
            barrier,
            inc=1,
            device_id=(lax.rem(me_dp + k, n_dp), me_mp),
            device_id_type=pl.DeviceIdType.MESH,
        )
    for k in range(1, n_mp):
        pl.semaphore_signal(
            barrier,
            inc=1,
            device_id=(me_dp, lax.rem(me_mp + k, n_mp)),
            device_id_type=pl.DeviceIdType.MESH,
        )
    lax.fori_loop(0, chunks, lambda c, _: kv_copy(c).start(), None)
    for copy in w_copies[1:]:
        copy.start()

    normed = rms_norm(hidden[...], attn_gain[...])
    w_copies[0].wait()
    own_query, own_key, own_value = (dot(normed, w_qkv[i]).astype(BF16) for i in range(3))
    appended[0] = own_key
    appended[1] = own_value
    queries[me_dp] = own_query
    pl.semaphore_wait(barrier, n_dp + n_mp - 2)

    def query_copy(k, slot):
        return pltpu.make_async_remote_copy(
            src_ref=queries.at[slot],
            dst_ref=queries.at[slot],
            send_sem=q_send.at[k],
            recv_sem=q_recv.at[k],
            device_id=(lax.rem(me_dp + k, n_dp), me_mp),
            device_id_type=pl.DeviceIdType.MESH,
        )

    for k in range(1, n_dp):
        query_copy(k, me_dp).start()

    owner_row = owners[...]
    owner_by_request = jnp.broadcast_to(owner_row, (requests, pages))
    member_rp = owner_by_request == lax.broadcasted_iota(jnp.int32, (requests, pages), 0)
    owner_by_page = jnp.transpose(owner_by_request.astype(F32))
    member_pr = owner_by_page == lax.broadcasted_iota(jnp.int32, (pages, requests), 1).astype(F32)
    page_length = jnp.sum(jnp.where(member_pr, lengths[...].astype(F32), 0.0), axis=1, keepdims=True)
    place = jnp.transpose(jnp.broadcast_to(places[...], (page_len, pages)).astype(F32))
    token = lax.broadcasted_iota(jnp.int32, (pages, page_len), 1).astype(F32)
    bias[...] = jnp.where(place * page_len + token < page_length, 0.0, NEGATIVE)

    lane = lax.broadcasted_iota(jnp.int32, (rows, LANES), 1)
    product = own_query.astype(F32) * own_key.astype(F32)
    self_lse = jnp.full((rows, LANES), NEGATIVE, F32)
    for h in range(heads):
        score = jnp.sum(product[:, h * HEAD_DIM : (h + 1) * HEAD_DIM], axis=1, keepdims=True)
        self_lse = jnp.where(lane == h, score * HEAD_DIM**-0.5, self_lse)

    for k in range(1, n_dp):
        query_copy(k, lax.rem(me_dp + n_dp - k, n_dp)).wait_recv()
    every_query = queries[...].reshape(requests, cols)
    page_query[...] = dot(member_pr.astype(F32).astype(BF16), every_query) * HEAD_DIM**-0.5

    head_mask = (
        lax.broadcasted_iota(jnp.int32, (8, cols), 1) // HEAD_DIM
        == lax.broadcasted_iota(jnp.int32, (8, cols), 0)
    ).astype(F32)
    half = lax.broadcasted_iota(jnp.int32, (8 * CHUNK, LANES), 1) < LANES // 2

    def visit(c, _):
        kv_copy(c).wait()
        at = pl.ds(c * CHUNK, CHUNK)
        chunk_query = page_query[at, :]
        chunk_bias = bias[at, :]
        dead = jnp.concatenate(
            [jnp.broadcast_to(chunk_bias[j : j + 1], (8, page_len)) for j in range(CHUNK)], axis=0
        )
        scores = jnp.concatenate(
            [
                lax.dot_general(
                    (chunk_query[j : j + 1] * head_mask).astype(BF16),
                    kv[0, c * CHUNK + j],
                    (((1,), (1,)), ((), ())),
                    preferred_element_type=F32,
                )
                for j in range(CHUNK)
            ],
            axis=0,
        ) + dead
        largest = jnp.max(scores, axis=1, keepdims=True)
        raw = jnp.where(dead < 0.0, 0.0, jnp.exp(scores - largest))
        total = jnp.sum(raw, axis=1, keepdims=True)
        page_stats[at] = jnp.where(half, largest, total).reshape(CHUNK, 8, LANES)
        weights = raw.astype(BF16)
        page_sum[at, :] = jnp.concatenate(
            [
                jnp.sum(
                    dot(weights[8 * j : 8 * j + 8], kv[1, c * CHUNK + j]) * head_mask,
                    axis=0,
                    keepdims=True,
                )
                for j in range(CHUNK)
            ],
            axis=0,
        )
        return None

    lax.fori_loop(0, chunks, visit, None)

    part = lax.broadcasted_iota(jnp.int32, (requests, cols), 1) // HEAD_DIM
    stat_lane = lax.broadcasted_iota(jnp.int32, (requests, LANES), 1)
    factor_part = lax.broadcasted_iota(jnp.int32, (cols, pages), 0) // HEAD_DIM
    factors = jnp.zeros((cols, pages), F32)
    inverse = jnp.zeros((requests, cols), F32)
    lse = jnp.full((requests, LANES), NEGATIVE, F32)
    for h in range(heads):
        stats = jnp.transpose(page_stats[:, h, :])
        max_row = stats[0:1, :]
        total_row = stats[LANES // 2 : LANES // 2 + 1, :]
        top = jnp.max(jnp.where(member_rp, max_row, NEGATIVE), axis=1, keepdims=True)
        top_row = jnp.sum(jnp.where(member_rp, top, 0.0), axis=0, keepdims=True)
        factor = jnp.where(owner_row >= 0, jnp.exp(jnp.minimum(max_row - top_row, 0.0)), 0.0)
        total = jnp.sum(jnp.where(member_rp, factor * total_row, 0.0), axis=1, keepdims=True)
        filled = total > 0.0
        safe = jnp.where(filled, total, 1.0)
        factors = jnp.where(factor_part == h, factor, factors)
        inverse = jnp.where(part == h, 1.0 / safe, inverse)
        lse = jnp.where(
            stat_lane == h, jnp.where(filled, top + jnp.log(safe), NEGATIVE), lse
        )
    scaled = page_sum[...] * jnp.transpose(factors)
    high = scaled.astype(BF16)
    low = (scaled - high.astype(F32)).astype(BF16)
    member = member_rp.astype(F32).astype(BF16)
    local = (dot(member, high) + dot(member, low)) * inverse
    partial_out[:, :, 0:cols] = local.reshape(n_dp, rows, cols)
    partial_out[:, :, cols : cols + LANES] = lse.reshape(n_dp, rows, LANES)

    def partial_copy(k):
        to = lax.rem(me_dp + k, n_dp)
        return pltpu.make_async_remote_copy(
            src_ref=partial_out.at[to],
            dst_ref=partial_in.at[k],
            send_sem=p_send.at[k],
            recv_sem=p_recv.at[k],
            device_id=(to, me_mp),
            device_id_type=pl.DeviceIdType.MESH,
        )

    for k in range(1, n_dp):
        partial_copy(k).start()
    partial_in[0] = partial_out[me_dp]
    for k in range(1, n_dp):
        partial_copy(k).wait_recv()

    lses = partial_in[:, :, cols : cols + LANES]
    top = jnp.maximum(self_lse, jnp.max(lses, axis=0))
    self_share = jnp.exp(self_lse - top)
    shares = jnp.exp(lses - top[None])
    total = self_share + jnp.sum(shares, axis=0)
    column = lax.broadcasted_iota(jnp.int32, (rows, cols), 1) // HEAD_DIM

    def widen(share):
        wide = jnp.zeros((rows, cols), F32)
        for h in range(heads):
            wide = jnp.where(column == h, share[:, h : h + 1], wide)
        return wide

    weighted = widen(self_share) * own_value.astype(F32)
    for k in range(n_dp):
        weighted = weighted + widen(shares[k]) * partial_in[k, :, 0:cols]
    context = (weighted / widen(total)).astype(BF16)

    def sum_over_mp(term, slots, at):
        slots[me_mp] = term.astype(BF16)

        def copy(k, slot):
            return pltpu.make_async_remote_copy(
                src_ref=slots.at[slot],
                dst_ref=slots.at[slot],
                send_sem=s_send.at[at, k],
                recv_sem=s_recv.at[at, k],
                device_id=(me_dp, lax.rem(me_mp + k, n_mp)),
                device_id_type=pl.DeviceIdType.MESH,
            )

        for k in range(1, n_mp):
            copy(k, me_mp).start()
        for k in range(1, n_mp):
            copy(k, lax.rem(me_mp + n_mp - k, n_mp)).wait_recv()
        for k in range(1, n_mp):
            copy(k, me_mp).wait_send()
        return jnp.sum(slots[...].astype(F32), axis=0)

    w_copies[1].wait()
    attended = sum_over_mp(dot(context, w_out[...]), sums_one, 0)
    residual = (hidden[...].astype(F32) + attended).astype(BF16)
    normed_mlp = rms_norm(residual, mlp_gain[...])

    tiles = width // LANES
    spread_from = lax.broadcasted_iota(jnp.int32, (LANES, 4 * LANES), 0)
    spread_to = lax.broadcasted_iota(jnp.int32, (LANES, 4 * LANES), 1)
    even = spread_to == 2 * spread_from
    odd = spread_to == 2 * LANES + 2 * spread_from + 1
    spread = (even | odd).astype(F32).astype(BF16)
    stacked = jnp.concatenate(
        [normed_mlp[:, i * LANES : (i + 1) * LANES] for i in range(tiles)], axis=0
    )
    apart = dot(stacked, spread).astype(BF16)
    w_copies[2].wait()
    gate_up = None
    for i in range(tiles):
        rows_i = apart[i * rows : (i + 1) * rows]
        left = jnp.concatenate([rows_i[:, : 2 * LANES], rows_i[:, 2 * LANES :]], axis=0)
        right = w_gu[i * LANES : (i + 1) * LANES].reshape(2 * LANES, w_gu.shape[2])
        step = dot(left, right)
        gate_up = step if gate_up is None else gate_up + step
    gate, up = gate_up[:rows], gate_up[rows:]
    activated = (gate / (1.0 + jnp.exp(-gate)) * up).astype(BF16)
    w_copies[3].wait()
    lowered = sum_over_mp(dot(activated, w_down[...]), sums_two, 1)
    hidden_out[...] = (residual.astype(F32) + lowered).astype(BF16)

    for k in range(1, n_dp):
        query_copy(k, me_dp).wait_send()
        partial_copy(k).wait_send()


def body(n_dp, n_mp, hidden, attn_gain, w_qkv, w_out, mlp_gain, w_gate_up, w_down, kv_cache, lengths, page_request, page_index):
    rows, width = hidden.shape
    cols = w_qkv.shape[2]
    pages, page_len = kv_cache.shape[1:3]
    vmem = pl.BlockSpec(memory_space=pltpu.VMEM)
    hbm = pl.BlockSpec(memory_space=pl.ANY)
    dma = pltpu.SemaphoreType.DMA
    w_qkv = jnp.transpose(w_qkv, (1, 0, 2))
    return pl.pallas_call(
        functools.partial(kernel, n_dp, n_mp),
        out_shape=(
            jax.ShapeDtypeStruct((2, rows, cols), BF16),
            jax.ShapeDtypeStruct((rows, width), BF16),
        ),
        in_specs=[vmem, vmem, hbm, hbm, vmem, hbm, hbm, hbm, vmem, vmem, vmem],
        out_specs=(vmem, vmem),
        scratch_shapes=[
            pltpu.VMEM(w_qkv.shape, BF16),
            pltpu.VMEM(w_out.shape, BF16),
            pltpu.VMEM(w_gate_up.shape, BF16),
            pltpu.VMEM(w_down.shape, BF16),
            pltpu.VMEM(kv_cache.shape, BF16),
            pltpu.VMEM((n_dp, rows, cols), BF16),
            pltpu.VMEM((n_dp, rows, cols + LANES), F32),
            pltpu.VMEM((n_dp, rows, cols + LANES), F32),
            pltpu.VMEM((n_mp, rows, width), BF16),
            pltpu.VMEM((n_mp, rows, width), BF16),
            pltpu.VMEM((pages, cols), F32),
            pltpu.VMEM((pages, page_len), F32),
            pltpu.VMEM((pages, 8, LANES), F32),
            pltpu.VMEM((pages, cols), F32),
            dma((4,)),
            dma((pages // CHUNK,)),
            dma((n_dp,)),
            dma((n_dp,)),
            dma((n_dp,)),
            dma((n_dp,)),
            dma((2, n_mp)),
            dma((2, n_mp)),
        ],
        compiler_params=pltpu.CompilerParams(
            collective_id=0, has_side_effects=True, vmem_limit_bytes=56 * 1024 * 1024
        ),
    )(
        hidden,
        attn_gain.reshape(1, width),
        w_qkv,
        w_out,
        mlp_gain.reshape(1, width),
        w_gate_up,
        w_down,
        kv_cache,
        lengths.reshape(1, -1),
        page_request.reshape(1, -1),
        page_index.reshape(1, -1),
    )


def solution(mesh):
    return jax.shard_map(
        functools.partial(body, mesh.shape["dp"], mesh.shape["mp"]),
        mesh=mesh,
        in_specs=(
            P("dp", None),
            P(),
            P(None, None, "mp"),
            P("mp", None),
            P(),
            P(None, None, "mp"),
            P("mp", None),
            P(None, "dp", None, "mp"),
            P(),
            P("dp"),
            P("dp"),
        ),
        out_specs=(P(None, "dp", "mp"), P("dp", None)),
        check_vma=False,
    )
```

```python
import functools

import jax
import jax.numpy as jnp
from jax import lax
from jax.experimental import pallas as pl
from jax.experimental.pallas import tpu as pltpu
from jax.sharding import PartitionSpec as P

HEAD_DIM = 64
CHUNK = 16
LANES = 128
EPSILON = 1e-05
NEGATIVE = -1e30
F32 = jnp.float32
BF16 = jnp.bfloat16


def rms_norm(values, gain):
    widened = values.astype(F32)
    mean_square = jnp.mean(widened * widened, axis=-1, keepdims=True)
    return (widened * lax.rsqrt(mean_square + EPSILON) * gain).astype(BF16)


def dot(a, b):
    return jnp.dot(a, b, preferred_element_type=F32)


def kernel(
    n_dp,
    n_mp,
    hidden,
    attn_gain,
    w_qkv_hbm,
    w_out_hbm,
    mlp_gain,
    w_gu_hbm,
    w_down_hbm,
    kv_hbm,
    lengths,
    owners,
    places,
    appended,
    hidden_out,
    w_qkv,
    w_out,
    w_gu,
    w_down,
    kv,
    queries,
    partial_out,
    partial_in,
    sums_one,
    sums_two,
    page_query,
    bias,
    page_stats,
    page_sum,
    w_sem,
    kv_sem,
    q_send,
    q_recv,
    p_send,
    p_recv,
    s_send,
    s_recv,
):
    rows, width = hidden.shape
    cols = w_qkv.shape[2]
    heads = cols // HEAD_DIM
    pages, page_len = kv.shape[1], kv.shape[2]
    requests = rows * n_dp
    chunks = pages // CHUNK
    me_dp = lax.axis_index("dp")
    me_mp = lax.axis_index("mp")

    w_copies = [
        pltpu.make_async_copy(src, dst, w_sem.at[i])
        for i, (src, dst) in enumerate(
            ((w_qkv_hbm, w_qkv), (w_out_hbm, w_out), (w_gu_hbm, w_gu), (w_down_hbm, w_down))
        )
    ]
    w_copies[0].start()

    def kv_copy(c):
        at = pl.ds(c * CHUNK, CHUNK)
        return pltpu.make_async_copy(kv_hbm.at[:, at], kv.at[:, at], kv_sem.at[c])

    barrier = pltpu.get_barrier_semaphore()
    for k in range(1, n_dp):
        pl.semaphore_signal(
            barrier,
            inc=1,
            device_id=(lax.rem(me_dp + k, n_dp), me_mp),
            device_id_type=pl.DeviceIdType.MESH,
        )
    for k in range(1, n_mp):
        pl.semaphore_signal(
            barrier,
            inc=1,
            device_id=(me_dp, lax.rem(me_mp + k, n_mp)),
            device_id_type=pl.DeviceIdType.MESH,
        )
    lax.fori_loop(0, chunks, lambda c, _: kv_copy(c).start(), None)
    for copy in w_copies[1:]:
        copy.start()

    normed = rms_norm(hidden[...], attn_gain[...])
    w_copies[0].wait()
    own_query, own_key, own_value = (dot(normed, w_qkv[i]).astype(BF16) for i in range(3))
    appended[0] = own_key
    appended[1] = own_value
    queries[me_dp] = own_query
    pl.semaphore_wait(barrier, n_dp + n_mp - 2)

    def query_copy(k, slot):
        return pltpu.make_async_remote_copy(
            src_ref=queries.at[slot],
            dst_ref=queries.at[slot],
            send_sem=q_send.at[k],
            recv_sem=q_recv.at[k],
            device_id=(lax.rem(me_dp + k, n_dp), me_mp),
            device_id_type=pl.DeviceIdType.MESH,
        )

    for k in range(1, n_dp):
        query_copy(k, me_dp).start()

    owner_row = owners[...]
    owner_by_request = jnp.broadcast_to(owner_row, (requests, pages))
    member_rp = owner_by_request == lax.broadcasted_iota(jnp.int32, (requests, pages), 0)
    owner_by_page = jnp.transpose(owner_by_request.astype(F32))
    member_pr = owner_by_page == lax.broadcasted_iota(jnp.int32, (pages, requests), 1).astype(F32)
    page_length = jnp.sum(jnp.where(member_pr, lengths[...].astype(F32), 0.0), axis=1, keepdims=True)
    place = jnp.transpose(jnp.broadcast_to(places[...], (page_len, pages)).astype(F32))
    token = lax.broadcasted_iota(jnp.int32, (pages, page_len), 1).astype(F32)
    bias[...] = jnp.where(place * page_len + token < page_length, 0.0, NEGATIVE)

    lane = lax.broadcasted_iota(jnp.int32, (rows, LANES), 1)
    product = own_query.astype(F32) * own_key.astype(F32)
    self_lse = jnp.full((rows, LANES), NEGATIVE, F32)
    for h in range(heads):
        score = jnp.sum(product[:, h * HEAD_DIM : (h + 1) * HEAD_DIM], axis=1, keepdims=True)
        self_lse = jnp.where(lane == h, score * HEAD_DIM**-0.5, self_lse)

    for k in range(1, n_dp):
        query_copy(k, lax.rem(me_dp + n_dp - k, n_dp)).wait_recv()
    every_query = queries[...].reshape(requests, cols)
    page_query[...] = dot(member_pr.astype(F32).astype(BF16), every_query) * HEAD_DIM**-0.5

    head_mask = (
        lax.broadcasted_iota(jnp.int32, (8, cols), 1) // HEAD_DIM
        == lax.broadcasted_iota(jnp.int32, (8, cols), 0)
    ).astype(F32)
    half = lax.broadcasted_iota(jnp.int32, (8 * CHUNK, LANES), 1) < LANES // 2

    def visit(c, _):
        kv_copy(c).wait()
        at = pl.ds(c * CHUNK, CHUNK)
        chunk_query = page_query[at, :]
        chunk_bias = bias[at, :]
        dead = jnp.concatenate(
            [jnp.broadcast_to(chunk_bias[j : j + 1], (8, page_len)) for j in range(CHUNK)], axis=0
        )
        scores = jnp.concatenate(
            [
                lax.dot_general(
                    (chunk_query[j : j + 1] * head_mask).astype(BF16),
                    kv[0, c * CHUNK + j],
                    (((1,), (1,)), ((), ())),
                    preferred_element_type=F32,
                )
                for j in range(CHUNK)
            ],
            axis=0,
        ) + dead
        largest = jnp.max(scores, axis=1, keepdims=True)
        raw = jnp.where(dead < 0.0, 0.0, jnp.exp(scores - largest))
        total = jnp.sum(raw, axis=1, keepdims=True)
        page_stats[at] = jnp.where(half, largest, total).reshape(CHUNK, 8, LANES)
        weights = raw.astype(BF16)
        page_sum[at, :] = jnp.concatenate(
            [
                jnp.sum(
                    dot(weights[8 * j : 8 * j + 8], kv[1, c * CHUNK + j]) * head_mask,
                    axis=0,
                    keepdims=True,
                )
                for j in range(CHUNK)
            ],
            axis=0,
        )
        return None

    lax.fori_loop(0, chunks, visit, None)

    part = lax.broadcasted_iota(jnp.int32, (requests, cols), 1) // HEAD_DIM
    stat_lane = lax.broadcasted_iota(jnp.int32, (requests, LANES), 1)
    factor_part = lax.broadcasted_iota(jnp.int32, (cols, pages), 0) // HEAD_DIM
    factors = jnp.zeros((cols, pages), F32)
    inverse = jnp.zeros((requests, cols), F32)
    lse = jnp.full((requests, LANES), NEGATIVE, F32)
    for h in range(heads):
        stats = jnp.transpose(page_stats[:, h, :])
        max_row = stats[0:1, :]
        total_row = stats[LANES // 2 : LANES // 2 + 1, :]
        top = jnp.max(jnp.where(member_rp, max_row, NEGATIVE), axis=1, keepdims=True)
        top_row = jnp.sum(jnp.where(member_rp, top, 0.0), axis=0, keepdims=True)
        factor = jnp.where(owner_row >= 0, jnp.exp(jnp.minimum(max_row - top_row, 0.0)), 0.0)
        total = jnp.sum(jnp.where(member_rp, factor * total_row, 0.0), axis=1, keepdims=True)
        filled = total > 0.0
        safe = jnp.where(filled, total, 1.0)
        factors = jnp.where(factor_part == h, factor, factors)
        inverse = jnp.where(part == h, 1.0 / safe, inverse)
        lse = jnp.where(
            stat_lane == h, jnp.where(filled, top + jnp.log(safe), NEGATIVE), lse
        )
    scaled = page_sum[...] * jnp.transpose(factors)
    high = scaled.astype(BF16)
    low = (scaled - high.astype(F32)).astype(BF16)
    member = member_rp.astype(F32).astype(BF16)
    local = (dot(member, high) + dot(member, low)) * inverse
    partial_out[:, :, 0:cols] = local.reshape(n_dp, rows, cols)
    partial_out[:, :, cols : cols + LANES] = lse.reshape(n_dp, rows, LANES)

    def partial_copy(k):
        to = lax.rem(me_dp + k, n_dp)
        return pltpu.make_async_remote_copy(
            src_ref=partial_out.at[to],
            dst_ref=partial_in.at[k],
            send_sem=p_send.at[k],
            recv_sem=p_recv.at[k],
            device_id=(to, me_mp),
            device_id_type=pl.DeviceIdType.MESH,
        )

    for k in range(1, n_dp):
        partial_copy(k).start()
    partial_in[0] = partial_out[me_dp]
    for k in range(1, n_dp):
        partial_copy(k).wait_recv()

    lses = partial_in[:, :, cols : cols + LANES]
    top = jnp.maximum(self_lse, jnp.max(lses, axis=0))
    self_share = jnp.exp(self_lse - top)
    shares = jnp.exp(lses - top[None])
    total = self_share + jnp.sum(shares, axis=0)
    column = lax.broadcasted_iota(jnp.int32, (rows, cols), 1) // HEAD_DIM

    def widen(share):
        wide = jnp.zeros((rows, cols), F32)
        for h in range(heads):
            wide = jnp.where(column == h, share[:, h : h + 1], wide)
        return wide

    weighted = widen(self_share) * own_value.astype(F32)
    for k in range(n_dp):
        weighted = weighted + widen(shares[k]) * partial_in[k, :, 0:cols]
    context = (weighted / widen(total)).astype(BF16)

    def sum_over_mp(term, slots, at):
        slots[me_mp] = term.astype(BF16)

        def copy(k, slot):
            return pltpu.make_async_remote_copy(
                src_ref=slots.at[slot],
                dst_ref=slots.at[slot],
                send_sem=s_send.at[at, k],
                recv_sem=s_recv.at[at, k],
                device_id=(me_dp, lax.rem(me_mp + k, n_mp)),
                device_id_type=pl.DeviceIdType.MESH,
            )

        for k in range(1, n_mp):
            copy(k, me_mp).start()
        for k in range(1, n_mp):
            copy(k, lax.rem(me_mp + n_mp - k, n_mp)).wait_recv()
        for k in range(1, n_mp):
            copy(k, me_mp).wait_send()
        return jnp.sum(slots[...].astype(F32), axis=0)

    w_copies[1].wait()
    attended = sum_over_mp(dot(context, w_out[...]), sums_one, 0)
    residual = (hidden[...].astype(F32) + attended).astype(BF16)
    normed_mlp = rms_norm(residual, mlp_gain[...])

    tiles = width // LANES
    spread_from = lax.broadcasted_iota(jnp.int32, (LANES, 4 * LANES), 0)
    spread_to = lax.broadcasted_iota(jnp.int32, (LANES, 4 * LANES), 1)
    even = spread_to == 2 * spread_from
    odd = spread_to == 2 * LANES + 2 * spread_from + 1
    spread = (even | odd).astype(F32).astype(BF16)
    stacked = jnp.concatenate(
        [normed_mlp[:, i * LANES : (i + 1) * LANES] for i in range(tiles)], axis=0
    )
    apart = dot(stacked, spread).astype(BF16)
    w_copies[2].wait()
    gate_up = None
    for i in range(tiles):
        rows_i = apart[i * rows : (i + 1) * rows]
        left = jnp.concatenate([rows_i[:, : 2 * LANES], rows_i[:, 2 * LANES :]], axis=0)
        right = w_gu[i * LANES : (i + 1) * LANES].reshape(2 * LANES, w_gu.shape[2])
        step = dot(left, right)
        gate_up = step if gate_up is None else gate_up + step
    gate, up = gate_up[:rows], gate_up[rows:]
    activated = (gate / (1.0 + jnp.exp(-gate)) * up).astype(BF16)
    w_copies[3].wait()
    lowered = sum_over_mp(dot(activated, w_down[...]), sums_two, 1)
    hidden_out[...] = (residual.astype(F32) + lowered).astype(BF16)

    for k in range(1, n_dp):
        query_copy(k, me_dp).wait_send()
        partial_copy(k).wait_send()


def body(n_dp, n_mp, hidden, attn_gain, w_qkv, w_out, mlp_gain, w_gate_up, w_down, kv_cache, lengths, page_request, page_index):
    rows, width = hidden.shape
    cols = w_qkv.shape[2]
    pages, page_len = kv_cache.shape[1:3]
    vmem = pl.BlockSpec(memory_space=pltpu.VMEM)
    hbm = pl.BlockSpec(memory_space=pl.ANY)
    dma = pltpu.SemaphoreType.DMA
    w_qkv = jnp.transpose(w_qkv, (1, 0, 2))
    return pl.pallas_call(
        functools.partial(kernel, n_dp, n_mp),
        out_shape=(
            jax.ShapeDtypeStruct((2, rows, cols), BF16),
            jax.ShapeDtypeStruct((rows, width), BF16),
        ),
        in_specs=[vmem, vmem, hbm, hbm, vmem, hbm, hbm, hbm, vmem, vmem, vmem],
        out_specs=(vmem, vmem),
        scratch_shapes=[
            pltpu.VMEM(w_qkv.shape, BF16),
            pltpu.VMEM(w_out.shape, BF16),
            pltpu.VMEM(w_gate_up.shape, BF16),
            pltpu.VMEM(w_down.shape, BF16),
            pltpu.VMEM(kv_cache.shape, BF16),
            pltpu.VMEM((n_dp, rows, cols), BF16),
            pltpu.VMEM((n_dp, rows, cols + LANES), F32),
            pltpu.VMEM((n_dp, rows, cols + LANES), F32),
            pltpu.VMEM((n_mp, rows, width), BF16),
            pltpu.VMEM((n_mp, rows, width), BF16),
            pltpu.VMEM((pages, cols), F32),
            pltpu.VMEM((pages, page_len), F32),
            pltpu.VMEM((pages, 8, LANES), F32),
            pltpu.VMEM((pages, cols), F32),
            dma((4,)),
            dma((pages // CHUNK,)),
            dma((n_dp,)),
            dma((n_dp,)),
            dma((n_dp,)),
            dma((n_dp,)),
            dma((2, n_mp)),
            dma((2, n_mp)),
        ],
        compiler_params=pltpu.CompilerParams(
            collective_id=0, has_side_effects=True, vmem_limit_bytes=56 * 1024 * 1024
        ),
    )(
        hidden,
        attn_gain.reshape(1, width),
        w_qkv,
        w_out,
        mlp_gain.reshape(1, width),
        w_gate_up,
        w_down,
        kv_cache,
        lengths.reshape(1, -1),
        page_request.reshape(1, -1),
        page_index.reshape(1, -1),
    )


def solution(mesh):
    return jax.shard_map(
        functools.partial(body, mesh.shape["dp"], mesh.shape["mp"]),
        mesh=mesh,
        in_specs=(
            P("dp", None),
            P(),
            P(None, None, "mp"),
            P("mp", None),
            P(),
            P(None, None, "mp"),
            P("mp", None),
            P(None, "dp", None, "mp"),
            P(),
            P("dp"),
            P("dp"),
        ),
        out_specs=(P(None, "dp", "mp"), P("dp", None)),
        check_vma=False,
    )
```
